32 devices in a mesh: section: 2 (over x), expert: 16 (over z, y, core).
Axes of the slice: x: 2, y: 2, z: 4, core: 2. Of those that a mesh axis runs over, the one named last changes fastest.
Arguments:
- hidden_in: bfloat16 [16, 128, 4096], P(None, 'expert'), may hold values from -6 to 6
- norm_gain: float32 [2, 4096], P('section'), may hold values from 0.5 to 2
- routes: int32 [2, 16, 128, 8], P('section', None, 'expert'), may hold values from 0 to 15, all different within a row; in each aligned block of 8 rows (0 to 7, 8 to 15, ..., all dimensions but the last counted through in order) at most 6 rows name the same one
- gate_codes: int32 [2, 16, 128, 8], P('section', None, 'expert'), may hold values from 1 to 255
- w_gate: bfloat16 [2, 16, 4096, 768], P('section', 'expert'), may hold values from -0.09375 to 0.09375
- w_up: bfloat16 [2, 16, 4096, 768], P('section', 'expert'), may hold values from -0.09375 to 0.09375
- w_down: bfloat16 [2, 16, 768, 4096], P('section', 'expert'), may hold values from -0.21875 to 0.21875
Outputs:
- stashed: bfloat16 [2, 16, 128, 4096], P('section', None, 'expert')
The draws below stay inside these ranges and needn't reach their ends.
Inputs may be any that keep to these rules, and one draw needn't show every extreme that they name: `routes`: each row names 8 different experts. Within each aligned block of 8 rows (the rows of one device for one layer and micro-batch), no expert is named by more than 6 rows, a bound that some block reaches.
All inputs are finite; a program needn't handle non-finite values.
Results may differ from the reference program's by a relative error of at most 0.025.
Values may be sent and summed in bfloat16 or wider, within the bound.
A program may use at most 64 MiB of HBM per device.

```python
import math
import jax
import jax.numpy as jnp
import numpy as np
from jax import lax

D = 4096
HID = 768
TOP = 8
ROWS = 8
MICRO = 16
EXPERTS = 16
LAYERS = 2
TOKENS = 128
CAP = 6
N_EXPERT = 16


def set_ends(drawn, key, low, top_value):
    shape = drawn.shape
    place = [jax.random.randint(jax.random.fold_in(key, axis), (), 0, shape[axis]) for axis in range(len(shape))]
    drawn = drawn.at[tuple(place)].set(low)
    longest = shape.index(max(shape))
    place[longest] = (place[longest] + 1) % shape[longest]
    return drawn.at[tuple(place)].set(top_value)


def shard_levels(stream_key, dims, pieces, low, top_value):
    def one(axis_at, parts):
        heights = jax.random.uniform(jax.random.fold_in(jax.random.fold_in(stream_key, 6), axis_at), (parts,), jnp.float32, low / len(pieces), top_value / len(pieces))
        return jnp.repeat(jnp.exp(heights), dims[axis_at] // parts).reshape((-1,) + (1,) * (len(dims) - axis_at - 1))

    gain = one(*pieces[0])
    for cut in pieces[1:]:
        gain = gain * one(*cut)
    return gain


def shared_out(rng, own, number, rows, amount, top, limit, lean):
    order = jax.random.permutation(rng, amount)
    crowded, usual = portions_of(amount, rows * top, limit, lean, True), portions_of(amount, rows * top, limit, lean, False)
    places = jnp.arange(amount)

    def named(sizes, rotation):
        used = int((sizes > 0).sum())
        fixed = max(1, used // 4)
        passed = fixed + (places - fixed + rotation * (used - fixed)) % max(1, amount - fixed)
        return jnp.zeros((amount,), jnp.int32).at[order[jnp.where(places < fixed, places, passed)]].set(jnp.asarray(sizes, jnp.int32))

    sizes = jnp.where(number % 4 == 0, named(crowded, number // 4), named(usual, number - number // 4 - 1))
    mixed = jax.random.permutation(jax.random.fold_in(own, 3), amount)
    donor, receiver = mixed[0:amount // 2 * 2:2], mixed[1:amount // 2 * 2:2]
    room = jnp.minimum(sizes[donor] - 1, limit - sizes[receiver]) // 2
    room = jnp.where((donor == order[0]) | (receiver == order[0]) | (sizes[receiver] == 0), 0, jnp.maximum(room, 0))
    passed = jax.random.randint(jax.random.fold_in(own, 4), (amount // 2,), 0, 1 << 20) % (room + 1)
    sizes = sizes.at[donor].add(-passed).at[receiver].add(passed)
    items = jnp.searchsorted(jnp.cumsum(sizes), jnp.arange(rows * top), side="right").astype(jnp.int32)
    listing = items.reshape(top, rows).T
    listing = listing[jax.random.permutation(jax.random.fold_in(own, 1), rows)]
    rotation = jax.random.randint(jax.random.fold_in(own, 2), (rows, 1), 0, top)
    return jnp.take_along_axis(listing, (jnp.arange(top)[None, :] + rotation) % top, axis=1)


def portions_of(count, total, limit, lean, full):
    loads = [(1 << 20) // math.isqrt(grade ** lean) + 1 for grade in range(1, count + 1)]
    largest = limit if full else min(limit, max(-(-total // count), total * loads[0] // sum(loads)))
    least = 1 if total - largest >= count - 1 else 0
    counts, spare = [largest] + [least] * (count - 1), total - largest - least * (count - 1)
    while spare > 0:
        movable = [i for i in range(1, count) if counts[i] < largest] or [i for i in range(1, count) if counts[i] < limit]
        pool, left = sum([loads[i] for i in movable]), spare
        for i in movable:
            addition = min(limit - counts[i], max(1, left * loads[i] // pool), spare)
            counts[i] = counts[i] + addition
            spare = spare - addition
    return np.array(counts)


def gaussian(stream_key, dims, deviation, bound, cuts=(), held_as=jnp.bfloat16):
    level = shard_levels(stream_key, dims, cuts, -0.22, 0.18) if cuts else 1.0
    result = jax.random.normal(stream_key, dims, jnp.float32) * deviation * level
    return jnp.minimum(jnp.maximum(result, -bound), bound).astype(held_as)


def setup_inputs(seed: int = 0) -> dict:
    arg_keys = jax.random.split(jax.random.key(seed), 8)
    hidden_in = gaussian(arg_keys[0], (MICRO, TOKENS, D), 1.0, 6.0, ((1, 16),))
    norm_gain = jnp.clip(0.5 + 1.5 * jax.random.uniform(arg_keys[1], (LAYERS, D), jnp.float32) ** shard_levels(arg_keys[1], (LAYERS, D), ((0, 2),), -0.2, 0.2), 0.5, 2.0)
    routes_keys = jax.random.split(jax.random.fold_in(arg_keys[2], 1), LAYERS * MICRO * TOKENS // ROWS)
    routes_turns = jax.random.permutation(jax.random.fold_in(arg_keys[2], 3), LAYERS * MICRO * TOKENS // ROWS)
    routes = jax.vmap(lambda own, number: shared_out(jax.random.fold_in(arg_keys[2], 2), own, number, ROWS, EXPERTS, TOP, CAP, 2))(routes_keys, routes_turns).reshape((LAYERS, MICRO, TOKENS, TOP))
    gate_codes = set_ends(jax.random.randint(arg_keys[3], (LAYERS, MICRO, TOKENS, TOP), 1, 256), jax.random.fold_in(arg_keys[3], 1), 1, 255).astype(jnp.int32)
    w_gate = gaussian(arg_keys[4], (LAYERS, EXPERTS, D, HID), D ** -0.5, 0.09375, ((0, 2), (1, 16)))
    w_up = gaussian(arg_keys[5], (LAYERS, EXPERTS, D, HID), D ** -0.5, 0.09375, ((0, 2), (1, 16)))
    w_down = gaussian(arg_keys[6], (LAYERS, EXPERTS, HID, D), HID ** -0.5, 0.21875, ((0, 2), (1, 16)))
    return {"hidden_in": hidden_in, "norm_gain": norm_gain, "routes": routes, "gate_codes": gate_codes, "w_gate": w_gate, "w_up": w_up, "w_down": w_down}


def slot_index(route_block):
    matches = (route_block[:, :, None] == jnp.arange(EXPERTS, dtype=jnp.int32)).astype(jnp.int32)
    flat_hits = matches.reshape(-1, EXPERTS)
    earlier = jnp.cumsum(flat_hits, axis=0) - flat_hits
    position = lax.optimization_barrier(jnp.sum(earlier * flat_hits, axis=1)).reshape(route_block.shape)
    return (route_block * CAP + position).astype(jnp.int32)

def expert_block(flat_rows, gate_matrix, up_matrix, down_matrix):
    gate_part = jnp.dot(flat_rows, gate_matrix, preferred_element_type=jnp.float32)
    up_part = jnp.dot(flat_rows, up_matrix, preferred_element_type=jnp.float32)
    activity = (jax.nn.silu(gate_part) * up_part).astype(jnp.bfloat16)
    return jnp.dot(activity, down_matrix, preferred_element_type=jnp.float32).astype(jnp.bfloat16)

def reference(hidden_in, norm_gain, routes, gate_codes, w_gate, w_up, w_down):
    current = hidden_in
    results = []
    blocks_count = MICRO * N_EXPERT
    for layer in range(LAYERS):
        floats = current.astype(jnp.float32)
        scale = lax.rsqrt(lax.optimization_barrier(jnp.mean(floats * floats, axis=-1, keepdims=True)) + 1e-06)
        normed = (floats * scale * norm_gain[layer]).astype(jnp.bfloat16)
        row_blocks = normed.reshape(blocks_count, ROWS, D)
        route_blocks = routes[layer].reshape(blocks_count, ROWS, TOP)
        codes = gate_codes[layer].reshape(blocks_count, ROWS, TOP).astype(jnp.float32)
        weights = codes / lax.optimization_barrier(jnp.sum(codes, axis=-1, keepdims=True))
        targets = jax.vmap(slot_index)(route_blocks)
        placing = lax.optimization_barrier(jnp.sum((targets[..., None] == jnp.arange(EXPERTS * CAP, dtype=jnp.int32)).astype(jnp.float32), axis=2))
        buffers = jnp.einsum('brs,brd->bsd', placing, row_blocks.astype(jnp.float32)).astype(jnp.bfloat16)
        per_expert = buffers.reshape(blocks_count, EXPERTS, CAP, D).transpose(1, 0, 2, 3).reshape(EXPERTS, blocks_count * CAP, D)

        def run_expert(operands):
            return expert_block(operands[0], operands[1], operands[2], operands[3])
        produced = lax.map(run_expert, (per_expert, w_gate[layer], w_up[layer], w_down[layer]))
        returned = produced.reshape(EXPERTS, blocks_count, CAP, D).transpose(1, 0, 2, 3).reshape(blocks_count, EXPERTS * CAP, D)
        picked = jax.vmap(lambda table, where_to: table[where_to])(returned, targets)
        mixed = lax.optimization_barrier(jnp.sum(weights[..., None] * picked.astype(jnp.float32), axis=2))
        current = (floats + mixed.reshape(MICRO, TOKENS, D)).astype(jnp.bfloat16)
        results.append(current)
    return jnp.stack(results)
```

```python
import jax
import jax.numpy as jnp
from jax import lax
from jax.sharding import PartitionSpec as P

GROUP = 2
LAG = 2


def per_device(hidden_in, norm_gain, routes, gate_codes, w_gate, w_up, w_down):
    experts = lax.axis_size("expert")
    sections = lax.axis_size("section")
    micro_count, rows, width = hidden_in.shape
    section_id = lax.axis_index("section")
    me = lax.axis_index("expert")
    gain = norm_gain[0]
    gate_matrix, up_matrix, down_matrix = w_gate[0, 0], w_up[0, 0], w_down[0, 0]
    chunks = micro_count // GROUP

    codes = gate_codes[0].astype(jnp.float32)
    weights = codes / jnp.sum(codes, axis=-1, keepdims=True)
    hits = routes[0][..., None] == jnp.arange(experts, dtype=jnp.int32)
    dense = jnp.sum(jnp.where(hits, weights[..., None], 0.0), axis=2)
    mine = lax.all_to_all(
        dense.transpose(2, 0, 1), "expert", split_axis=0, concat_axis=0, tiled=True
    )
    mine = mine.transpose(1, 0, 2)

    stash = jnp.zeros((micro_count, rows, width), jnp.bfloat16)
    outs = []
    for step in range(chunks + LAG * (sections - 1)):
        chunk = step - LAG * section_id
        active = jnp.logical_and(chunk >= 0, chunk < chunks)
        at = jnp.clip(chunk, 0, chunks - 1) * GROUP
        layer_in = lax.dynamic_slice_in_dim(hidden_in, at, GROUP, 0)
        if step >= LAG:
            incoming = lax.ppermute(
                outs[step - LAG], "section", [(s, s + 1) for s in range(sections - 1)]
            )
            layer_in = jnp.where(section_id == 0, layer_in, incoming)
        floats = layer_in.astype(jnp.float32)
        scale = lax.rsqrt(jnp.mean(floats * floats, axis=-1, keepdims=True) + 1e-06)
        normed = (floats * scale * gain).astype(jnp.bfloat16)
        gathered = lax.all_gather(
            normed.reshape(GROUP * rows, width), "expert", axis=0, tiled=True
        )
        gate_part = jnp.dot(gathered, gate_matrix, preferred_element_type=jnp.float32)
        up_part = jnp.dot(gathered, up_matrix, preferred_element_type=jnp.float32)
        act = (jax.nn.silu(gate_part) * up_part).astype(jnp.bfloat16)
        w = lax.dynamic_slice_in_dim(mine, at, GROUP, 0).transpose(1, 0, 2).reshape(-1, 1)
        part = jnp.dot(act, down_matrix, preferred_element_type=jnp.float32) * w
        mixed = lax.psum_scatter(
            part.astype(jnp.bfloat16), "expert", scatter_dimension=0, tiled=True
        )
        out = (floats + mixed.astype(jnp.float32).reshape(floats.shape)).astype(jnp.bfloat16)
        outs.append(out)
        old = lax.dynamic_slice_in_dim(stash, at, GROUP, 0)
        stash = lax.dynamic_update_slice_in_dim(stash, jnp.where(active, out, old), at, 0)
    return stash[None]


def solution(mesh):
    return jax.shard_map(
        per_device,
        mesh=mesh,
        in_specs=(
            P(None, "expert", None),
            P("section", None),
            P("section", None, "expert", None),
            P("section", None, "expert", None),
            P("section", "expert", None, None),
            P("section", "expert", None, None),
            P("section", "expert", None, None),
        ),
        out_specs=P("section", None, "expert", None),
        check_vma=False,
    )
```

```python
import functools

import jax
import jax.numpy as jnp
from jax import lax
from jax.experimental import pallas as pl
from jax.experimental.pallas import tpu as pltpu
from jax.sharding import PartitionSpec as P

MESH = pl.DeviceIdType.MESH
ROWS = 16


def moe_kernel(sections, line, hidden, gain, mine, wg, wu, wd, out,
               X, G, A, Pt, RC, RY, RZ, Q,
               x_send, x_recv, az_send, az_recv, ay_send, ay_recv, ac_send, ac_recv,
               rc_send, rc_recv, ry_send, ry_recv, rz_send, rz_recv):
    chunks, _, width = hidden.shape
    hid = wg.shape[1]
    s = lax.axis_index("section")
    e = lax.axis_index("expert")
    c = lax.rem(e, 2)
    y = lax.rem(e // 2, 2)
    z = e // 4

    def dev(zz, yy, cc):
        return (s, (zz * 2 + yy) * 2 + cc)

    sibling = dev(z, y, 1 - c)
    across = dev(z, 1 - y, c)
    others = [dev(lax.rem(z + i, line), y, c) for i in range(1, line)]
    here = y * line + z

    barrier = pltpu.get_barrier_semaphore()
    for d in [sibling, across] + others:
        pl.semaphore_signal(barrier, inc=1, device_id=d, device_id_type=MESH)

    @pl.when(s > 0)
    def _():
        pl.semaphore_signal(barrier, inc=1, device_id=(s - 1, e), device_id_type=MESH)

    @pl.when(s < sections - 1)
    def _():
        pl.semaphore_signal(barrier, inc=1, device_id=(s + 1, e), device_id_type=MESH)

    first = (s == 0).astype(jnp.int32)
    last = (s == sections - 1).astype(jnp.int32)
    pl.semaphore_wait(barrier, line + 3 - first - last)

    def remote(src, dst, send, recv, device):
        return pltpu.make_async_remote_copy(
            src_ref=src, dst_ref=dst, send_sem=send, recv_sem=recv,
            device_id=device, device_id_type=MESH)

    def az(k):
        a = lax.rem(k, 3)
        return [remote(G.at[a, c, here], G.at[a, c, here], az_send.at[a, i], az_recv.at[a, i], others[i])
                for i in range(line - 1)]

    def ay(k):
        a = lax.rem(k, 3)
        half = pl.ds(y * line, line)
        return remote(G.at[a, c, half], G.at[a, c, half], ay_send.at[a], ay_recv.at[a], across)

    def ac(k):
        a = lax.rem(k, 3)
        return remote(G.at[a, c], G.at[a, c], ac_send.at[a], ac_recv.at[a], sibling)

    def rc(k):
        b = lax.rem(k, 2)
        return remote(Pt.at[1 - c], RC.at[b], rc_send.at[b], rc_recv.at[b], sibling)

    def ry(k):
        b = lax.rem(k, 2)
        return remote(Q.at[pl.ds((1 - y) * line, line)], RY.at[b], ry_send.at[b], ry_recv.at[b], across)

    def rz(k):
        b = lax.rem(k, 2)
        return [remote(Q.at[y * line + lax.rem(z + i, line)], RZ.at[b, i - 1],
                       rz_send.at[b, i - 1], rz_recv.at[b, i - 1], others[i - 1])
                for i in range(1, line)]

    def xs(r):
        return remote(out.at[r], X.at[r], x_send, x_recv.at[r], (s + 1, e))

    def step(k, carry):
        gather = k < chunks
        work = jnp.logical_and(k >= 1, k <= chunks)
        back = k >= 2
        r = k - 2
        b = lax.rem(k, 2)

        @pl.when(back)
        def _():
            rc(k).start()

        @pl.when(gather)
        def _():
            @pl.when(s == 0)
            def _():
                X[k] = hidden[k]

            @pl.when(s > 0)
            def _():
                remote(out.at[k], X.at[k], x_send, x_recv.at[k], (s - 1, e)).wait_recv()

            v = X[k].astype(jnp.float32)
            scale = lax.rsqrt(jnp.mean(v * v, axis=-1, keepdims=True) + 1e-06)
            G[lax.rem(k, 3), c, here] = (v * scale * gain[...]).astype(jnp.bfloat16)
            for copy in az(k):
                copy.start()

        @pl.when(back)
        def _():
            rc(k).wait()

            def add(i, carry):
                Q[i] = (Pt[c, i].astype(jnp.float32) + RC[b, i].astype(jnp.float32)).astype(jnp.bfloat16)
                return carry

            lax.fori_loop((1 - y) * line, (1 - y) * line + line, add, 0)
            ry(k).start()
            lax.fori_loop(y * line, y * line + line, add, 0)

        @pl.when(work)
        def _():
            def up(j, carry):
                cols = pl.ds(pl.multiple_of(j * 256, 256), 256)
                rows = G[lax.rem(k - 1, 3)].reshape(-1, width)
                g = jnp.dot(rows, wg[:, cols], preferred_element_type=jnp.float32)
                u = jnp.dot(rows, wu[:, cols], preferred_element_type=jnp.float32)
                A[:, cols] = (g / (1.0 + jnp.exp(-g)) * u).astype(jnp.bfloat16)
                return carry

            lax.fori_loop(0, hid // 256, up, 0)

        @pl.when(gather)
        def _():
            for copy in az(k):
                copy.wait()
            ay(k).start()

        @pl.when(back)
        def _():
            ry(k).wait()

            def add(i, carry):
                j = y * line + i
                Q[j] = (Q[j].astype(jnp.float32) + RY[b, i].astype(jnp.float32)).astype(jnp.bfloat16)
                return carry

            lax.fori_loop(0, line, add, 0)
            for copy in rz(k):
                copy.start()

        @pl.when(work)
        def _():
            def down(j, carry):
                cols = pl.ds(pl.multiple_of(j * 256, 256), 256)
                p = jnp.dot(A[...], wd[:, cols], preferred_element_type=jnp.float32) * mine[k - 1]
                Pt[:, :, :, cols] = p.astype(jnp.bfloat16).reshape(2, 2 * line, ROWS, 256)
                return carry

            lax.fori_loop(0, width // 256, down, 0)

        @pl.when(gather)
        def _():
            ay(k).wait()
            ac(k).start()

        @pl.when(back)
        def _():
            for copy in rz(k):
                copy.wait()
            total = Q[here].astype(jnp.float32)
            for i in range(line - 1):
                total = total + RZ[b, i].astype(jnp.float32)
            out[r] = (X[r].astype(jnp.float32) + total).astype(jnp.bfloat16)

            @pl.when(s < sections - 1)
            def _():
                xs(r).start()

        @pl.when(gather)
        def _():
            ac(k).wait()

        @pl.when(jnp.logical_and(back, s < sections - 1))
        def _():
            xs(r).wait_send()

        return carry

    lax.fori_loop(0, chunks + 2, step, 0)


def per_device(hidden_in, norm_gain, routes, gate_codes, w_gate, w_up, w_down):
    experts = lax.axis_size("expert")
    sections = lax.axis_size("section")
    micro_count, rows, width = hidden_in.shape
    line = experts // 4
    group = ROWS // rows
    chunks = micro_count // group
    hid = w_gate.shape[-1]

    codes = gate_codes[0].astype(jnp.float32)
    weights = codes / jnp.sum(codes, axis=-1, keepdims=True)
    hits = routes[0][..., None] == jnp.arange(experts, dtype=jnp.int32)
    dense = jnp.sum(jnp.where(hits, weights[..., None], 0.0), axis=2)
    mine = lax.all_to_all(
        dense.transpose(2, 0, 1), "expert", split_axis=0, concat_axis=0, tiled=True
    )
    mine = mine.reshape(line, 2, 2, chunks, ROWS).transpose(3, 2, 1, 0, 4)
    mine = mine.reshape(chunks, experts * ROWS, 1)

    bf = jnp.bfloat16
    dma = pltpu.SemaphoreType.DMA
    out = pl.pallas_call(
        functools.partial(moe_kernel, sections, line),
        out_shape=jax.ShapeDtypeStruct((chunks, ROWS, width), bf),
        in_specs=[pl.BlockSpec(memory_space=pltpu.VMEM)] * 6,
        out_specs=pl.BlockSpec(memory_space=pltpu.VMEM),
        scratch_shapes=[
            pltpu.VMEM((chunks, ROWS, width), bf),
            pltpu.VMEM((3, 2, 2 * line, ROWS, width), bf),
            pltpu.VMEM((experts * ROWS, hid), bf),
            pltpu.VMEM((2, 2 * line, ROWS, width), bf),
            pltpu.VMEM((2, 2 * line, ROWS, width), bf),
            pltpu.VMEM((2, line, ROWS, width), bf),
            pltpu.VMEM((2, line - 1, ROWS, width), bf),
            pltpu.VMEM((2 * line, ROWS, width), bf),
            dma, dma((chunks,)),
            dma((3, line - 1)), dma((3, line - 1)),
            dma((3,)), dma((3,)), dma((3,)), dma((3,)),
            dma((2,)), dma((2,)), dma((2,)), dma((2,)),
            dma((2, line - 1)), dma((2, line - 1)),
        ],
        compiler_params=pltpu.CompilerParams(
            collective_id=0, has_side_effects=True, vmem_limit_bytes=56 * 2**20
        ),
        cost_estimate=pl.CostEstimate(
            flops=6 * chunks * experts * ROWS * width * hid,
            bytes_accessed=6 * width * hid, transcendentals=0),
    )(hidden_in.reshape(chunks, ROWS, width), norm_gain, mine, w_gate[0, 0], w_up[0, 0], w_down[0, 0])
    return out.reshape(1, micro_count, rows, width)


def solution(mesh):
    return jax.shard_map(
        per_device,
        mesh=mesh,
        in_specs=(
            P(None, "expert", None),
            P("section", None),
            P("section", None, "expert", None),
            P("section", None, "expert", None),
            P("section", "expert", None, None),
            P("section", "expert", None, None),
            P("section", "expert", None, None),
        ),
        out_specs=P("section", None, "expert", None),
        check_vma=False,
    )
```

```python
import functools

import jax
import jax.numpy as jnp
from jax import lax
from jax.experimental import pallas as pl
from jax.experimental.pallas import tpu as pltpu
from jax.sharding import PartitionSpec as P

MESH = pl.DeviceIdType.MESH
ROWS = 16


def moe_kernel(sections, line, hidden, gain, mine, wg, wu, wd, out,
               X, G, A, Pt, RC, RY, RZ, Q,
               x_send, x_recv, az_send, az_recv, ay_send, ay_recv, ac_send, ac_recv,
               rc_send, rc_recv, ry_send, ry_recv, rz_send, rz_recv):
    chunks, _, width = hidden.shape
    hid = wg.shape[1]
    s = lax.axis_index("section")
    e = lax.axis_index("expert")
    c = lax.rem(e, 2)
    y = lax.rem(e // 2, 2)
    z = e // 4

    def dev(zz, yy, cc):
        return (s, (zz * 2 + yy) * 2 + cc)

    sibling = dev(z, y, 1 - c)
    across = dev(z, 1 - y, c)
    others = [dev(lax.rem(z + i, line), y, c) for i in range(1, line)]
    here = y * line + z

    barrier = pltpu.get_barrier_semaphore()
    for d in [sibling, across] + others:
        pl.semaphore_signal(barrier, inc=1, device_id=d, device_id_type=MESH)

    @pl.when(s > 0)
    def _():
        pl.semaphore_signal(barrier, inc=1, device_id=(s - 1, e), device_id_type=MESH)

    @pl.when(s < sections - 1)
    def _():
        pl.semaphore_signal(barrier, inc=1, device_id=(s + 1, e), device_id_type=MESH)

    first = (s == 0).astype(jnp.int32)
    last = (s == sections - 1).astype(jnp.int32)
    pl.semaphore_wait(barrier, line + 3 - first - last)

    def remote(src, dst, send, recv, device):
        return pltpu.make_async_remote_copy(
            src_ref=src, dst_ref=dst, send_sem=send, recv_sem=recv,
            device_id=device, device_id_type=MESH)

    def az(k):
        a = lax.rem(k, 3)
        return [remote(G.at[a, c, here], G.at[a, c, here], az_send.at[a, i], az_recv.at[a, i], others[i])
                for i in range(line - 1)]

    def ay(k):
        a = lax.rem(k, 3)
        half = pl.ds(y * line, line)
        return remote(G.at[a, c, half], G.at[a, c, half], ay_send.at[a], ay_recv.at[a], across)

    def ac(k):
        a = lax.rem(k, 3)
        return remote(G.at[a, c], G.at[a, c], ac_send.at[a], ac_recv.at[a], sibling)

    def rc(k):
        b = lax.rem(k, 2)
        return remote(Pt.at[1 - c], RC.at[b], rc_send.at[b], rc_recv.at[b], sibling)

    def ry(k):
        b = lax.rem(k, 2)
        return remote(Q.at[pl.ds((1 - y) * line, line)], RY.at[b], ry_send.at[b], ry_recv.at[b], across)

    def rz(k):
        b = lax.rem(k, 2)
        return [remote(Q.at[y * line + lax.rem(z + i, line)], RZ.at[b, i - 1],
                       rz_send.at[b, i - 1], rz_recv.at[b, i - 1], others[i - 1])
                for i in range(1, line)]

    def xs(r):
        return remote(out.at[r], X.at[r], x_send, x_recv.at[r], (s + 1, e))

    def step(k, carry):
        gather = k < chunks
        work = jnp.logical_and(k >= 1, k <= chunks)
        back = k >= 2
        r = k - 2
        b = lax.rem(k, 2)

        @pl.when(gather)
        def _():
            @pl.when(s == 0)
            def _():
                X[k] = hidden[k]

            @pl.when(s > 0)
            def _():
                remote(out.at[k], X.at[k], x_send, x_recv.at[k], (s - 1, e)).wait_recv()

            v = X[k].astype(jnp.float32)
            scale = lax.rsqrt(jnp.mean(v * v, axis=-1, keepdims=True) + 1e-06)
            G[lax.rem(k, 3), c, here] = (v * scale * gain[...]).astype(jnp.bfloat16)
            for copy in az(k):
                copy.start()

        @pl.when(back)
        def _():
            rc(k).wait()

            def add(i, carry):
                Q[i] = (Pt[c, i].astype(jnp.float32) + RC[b, i].astype(jnp.float32)).astype(jnp.bfloat16)
                return carry

            lax.fori_loop((1 - y) * line, (1 - y) * line + line, add, 0)
            ry(k).start()
            lax.fori_loop(y * line, y * line + line, add, 0)

        @pl.when(work)
        def _():
            def up(j, carry):
                cols = pl.ds(pl.multiple_of(j * 256, 256), 256)
                rows = G[lax.rem(k - 1, 3)].reshape(-1, width)
                g = jnp.dot(rows, wg[:, cols], preferred_element_type=jnp.float32)
                u = jnp.dot(rows, wu[:, cols], preferred_element_type=jnp.float32)
                A[:, cols] = (g / (1.0 + jnp.exp(-g)) * u).astype(jnp.bfloat16)
                return carry

            ac(k - 1).wait()
            lax.fori_loop(0, hid // 256, up, 0)

        @pl.when(gather)
        def _():
            for copy in az(k):
                copy.wait()
            ay(k).start()

        @pl.when(back)
        def _():
            ry(k).wait()

            def add(i, carry):
                j = y * line + i
                Q[j] = (Q[j].astype(jnp.float32) + RY[b, i].astype(jnp.float32)).astype(jnp.bfloat16)
                return carry

            lax.fori_loop(0, line, add, 0)
            for copy in rz(k):
                copy.start()

        @pl.when(work)
        def _():
            def down(j, carry):
                cols = pl.ds(pl.multiple_of(j * 256, 256), 256)
                p = jnp.dot(A[...], wd[:, cols], preferred_element_type=jnp.float32) * mine[k - 1]
                Pt[:, :, :, cols] = p.astype(jnp.bfloat16).reshape(2, 2 * line, ROWS, 256)
                return carry

            lax.fori_loop(0, width // 256, down, 0)
            rc(k + 1).start()

        @pl.when(gather)
        def _():
            ay(k).wait()
            ac(k).start()

        @pl.when(back)
        def _():
            for copy in rz(k):
                copy.wait()
            total = Q[here].astype(jnp.float32)
            for i in range(line - 1):
                total = total + RZ[b, i].astype(jnp.float32)
            out[r] = (X[r].astype(jnp.float32) + total).astype(jnp.bfloat16)

            @pl.when(s < sections - 1)
            def _():
                xs(r).start()

        @pl.when(jnp.logical_and(back, s < sections - 1))
        def _():
            xs(r).wait_send()

        return carry

    lax.fori_loop(0, chunks + 2, step, 0)


def per_device(hidden_in, norm_gain, routes, gate_codes, w_gate, w_up, w_down):
    experts = lax.axis_size("expert")
    sections = lax.axis_size("section")
    micro_count, rows, width = hidden_in.shape
    line = experts // 4
    group = ROWS // rows
    chunks = micro_count // group
    hid = w_gate.shape[-1]

    codes = gate_codes[0].astype(jnp.float32)
    weights = codes / jnp.sum(codes, axis=-1, keepdims=True)
    hits = routes[0][..., None] == jnp.arange(experts, dtype=jnp.int32)
    dense = jnp.sum(jnp.where(hits, weights[..., None], 0.0), axis=2)
    mine = lax.all_to_all(
        dense.transpose(2, 0, 1), "expert", split_axis=0, concat_axis=0, tiled=True
    )
    mine = mine.reshape(line, 2, 2, chunks, ROWS).transpose(3, 2, 1, 0, 4)
    mine = mine.reshape(chunks, experts * ROWS, 1)

    bf = jnp.bfloat16
    dma = pltpu.SemaphoreType.DMA
    out = pl.pallas_call(
        functools.partial(moe_kernel, sections, line),
        out_shape=jax.ShapeDtypeStruct((chunks, ROWS, width), bf),
        in_specs=[pl.BlockSpec(memory_space=pltpu.VMEM)] * 6,
        out_specs=pl.BlockSpec(memory_space=pltpu.VMEM),
        scratch_shapes=[
            pltpu.VMEM((chunks, ROWS, width), bf),
            pltpu.VMEM((3, 2, 2 * line, ROWS, width), bf),
            pltpu.VMEM((experts * ROWS, hid), bf),
            pltpu.VMEM((2, 2 * line, ROWS, width), bf),
            pltpu.VMEM((2, 2 * line, ROWS, width), bf),
            pltpu.VMEM((2, line, ROWS, width), bf),
            pltpu.VMEM((2, line - 1, ROWS, width), bf),
            pltpu.VMEM((2 * line, ROWS, width), bf),
            dma, dma((chunks,)),
            dma((3, line - 1)), dma((3, line - 1)),
            dma((3,)), dma((3,)), dma((3,)), dma((3,)),
            dma((2,)), dma((2,)), dma((2,)), dma((2,)),
            dma((2, line - 1)), dma((2, line - 1)),
        ],
        compiler_params=pltpu.CompilerParams(
            collective_id=0, has_side_effects=True, vmem_limit_bytes=56 * 2**20
        ),
        cost_estimate=pl.CostEstimate(
            flops=6 * chunks * experts * ROWS * width * hid,
            bytes_accessed=6 * width * hid, transcendentals=0),
    )(hidden_in.reshape(chunks, ROWS, width), norm_gain, mine, w_gate[0, 0], w_up[0, 0], w_down[0, 0])
    return out.reshape(1, micro_count, rows, width)


def solution(mesh):
    return jax.shard_map(
        per_device,
        mesh=mesh,
        in_specs=(
            P(None, "expert", None),
            P("section", None),
            P("section", None, "expert", None),
            P("section", None, "expert", None),
            P("section", "expert", None, None),
            P("section", "expert", None, None),
            P("section", "expert", None, None),
        ),
        out_specs=P("section", None, "expert", None),
        check_vma=False,
    )
```

```python
import functools

import jax
import jax.numpy as jnp
from jax import lax
from jax.experimental import pallas as pl
from jax.experimental.pallas import tpu as pltpu
from jax.sharding import PartitionSpec as P

MESH = pl.DeviceIdType.MESH
ROWS = 16
LANES = 128


def moe_kernel(sections, line, hidden, gain, codes, wg_hbm, wu_hbm, wd_hbm, out,
               wg, wu, wd, w_sem,
               X, G, A, Pt, RC, RY, RZ, Q,
               x_send, x_recv, az_send, az_recv, ay_send, ay_recv, ac_send, ac_recv,
               rc_send, rc_recv, ry_send, ry_recv, rz_send, rz_recv):
    chunks, _, width = hidden.shape
    hid = wg.shape[1]
    s = lax.axis_index("section")
    e = lax.axis_index("expert")
    c = lax.rem(e, 2)
    y = lax.rem(e // 2, 2)
    z = e // 4

    def dev(zz, yy, cc):
        return (s, (zz * 2 + yy) * 2 + cc)

    sibling = dev(z, y, 1 - c)
    across = dev(z, 1 - y, c)
    others = [dev(lax.rem(z + i, line), y, c) for i in range(1, line)]
    here = y * line + z

    barrier = pltpu.get_barrier_semaphore()
    for d in [sibling, across] + others:
        pl.semaphore_signal(barrier, inc=1, device_id=d, device_id_type=MESH)

    @pl.when(s > 0)
    def _():
        pl.semaphore_signal(barrier, inc=1, device_id=(s - 1, e), device_id_type=MESH)

    @pl.when(s < sections - 1)
    def _():
        pl.semaphore_signal(barrier, inc=1, device_id=(s + 1, e), device_id_type=MESH)

    first = (s == 0).astype(jnp.int32)
    last = (s == sections - 1).astype(jnp.int32)
    pl.semaphore_wait(barrier, line + 3 - first - last)

    def remote(src, dst, send, recv, device):
        return pltpu.make_async_remote_copy(
            src_ref=src, dst_ref=dst, send_sem=send, recv_sem=recv,
            device_id=device, device_id_type=MESH)

    loads = [pltpu.make_async_copy(src, dst, w_sem.at[i])
             for i, (src, dst) in enumerate(((wg_hbm, wg), (wu_hbm, wu), (wd_hbm, wd)))]
    for load in loads:
        load.start()

    def az(k):
        a = lax.rem(k, 3)
        return [remote(G.at[a, c, here], G.at[a, c, here], az_send.at[a, i], az_recv.at[a, i], others[i])
                for i in range(line - 1)]

    def ay(k):
        a = lax.rem(k, 3)
        half = pl.ds(y * line, line)
        return remote(G.at[a, c, half], G.at[a, c, half], ay_send.at[a], ay_recv.at[a], across)

    def ac(k):
        a = lax.rem(k, 3)
        return remote(G.at[a, c], G.at[a, c], ac_send.at[a], ac_recv.at[a], sibling)

    def rc(k):
        b = lax.rem(k, 2)
        return remote(Pt.at[1 - c], RC.at[b], rc_send.at[b], rc_recv.at[b], sibling)

    def ry(k):
        b = lax.rem(k, 2)
        return remote(Q.at[pl.ds((1 - y) * line, line)], RY.at[b], ry_send.at[b], ry_recv.at[b], across)

    def rz(k):
        b = lax.rem(k, 2)
        return [remote(Q.at[y * line + lax.rem(z + i, line)], RZ.at[b, i - 1],
                       rz_send.at[b, i - 1], rz_recv.at[b, i - 1], others[i - 1])
                for i in range(1, line)]

    def xs(r):
        return remote(out.at[r], X.at[r], x_send, x_recv.at[r], (s + 1, e))

    def step(k, carry):
        gather = k < chunks
        work = jnp.logical_and(k >= 1, k <= chunks)
        back = k >= 2
        r = k - 2
        b = lax.rem(k, 2)

        @pl.when(gather)
        def _():
            @pl.when(s == 0)
            def _():
                X[k] = hidden[k]

            @pl.when(s > 0)
            def _():
                remote(out.at[k], X.at[k], x_send, x_recv.at[k], (s - 1, e)).wait_recv()

            v = X[k].astype(jnp.float32)
            scale = lax.rsqrt(jnp.mean(v * v, axis=-1, keepdims=True) + 1e-06)
            G[lax.rem(k, 3), c, here, :, :width] = (v * scale * gain[...]).astype(jnp.bfloat16)
            G[lax.rem(k, 3), c, here, :, width:] = codes[k]
            for copy in az(k):
                copy.start()

        @pl.when(back)
        def _():
            rc(k).wait()

            def add(i, carry):
                Q[i] = (Pt[c, i].astype(jnp.float32) + RC[b, i].astype(jnp.float32)).astype(jnp.bfloat16)
                return carry

            lax.fori_loop((1 - y) * line, (1 - y) * line + line, add, 0)
            ry(k).start()
            lax.fori_loop(y * line, y * line + line, add, 0)

        @pl.when(work)
        def _():
            def up(j, carry):
                cols = pl.ds(pl.multiple_of(j * 256, 256), 256)
                rows = G[lax.rem(k - 1, 3), :, :, :, :width].reshape(-1, width)
                g = jnp.dot(rows, wg[:, cols], preferred_element_type=jnp.float32)
                u = jnp.dot(rows, wu[:, cols], preferred_element_type=jnp.float32)
                A[:, cols] = (g / (1.0 + jnp.exp(-g)) * u).astype(jnp.bfloat16)
                return carry

            @pl.when(k == 1)
            def _():
                for load in loads:
                    load.wait()

            ac(k - 1).wait()
            lax.fori_loop(0, hid // 256, up, 0)

        @pl.when(gather)
        def _():
            for copy in az(k):
                copy.wait()
            ay(k).start()

        @pl.when(back)
        def _():
            ry(k).wait()

            def add(i, carry):
                j = y * line + i
                Q[j] = (Q[j].astype(jnp.float32) + RY[b, i].astype(jnp.float32)).astype(jnp.bfloat16)
                return carry

            lax.fori_loop(0, line, add, 0)
            for copy in rz(k):
                copy.start()

        @pl.when(work)
        def _():
            parts = G[lax.rem(k - 1, 3), :, :, :, width:].reshape(-1, LANES).astype(jnp.float32)
            lane = lax.broadcasted_iota(jnp.int32, parts.shape, 1)
            own = jnp.sum(jnp.where(lane == e, parts, 0.0), axis=1, keepdims=True)
            mine = own / jnp.sum(parts, axis=1, keepdims=True)

            def down(j, carry):
                cols = pl.ds(pl.multiple_of(j * 256, 256), 256)
                p = jnp.dot(A[...], wd[:, cols], preferred_element_type=jnp.float32) * mine
                Pt[:, :, :, cols] = p.astype(jnp.bfloat16).reshape(2, 2 * line, ROWS, 256)
                return carry

            lax.fori_loop(0, width // 256, down, 0)
            rc(k + 1).start()

        @pl.when(gather)
        def _():
            ay(k).wait()
            ac(k).start()

        @pl.when(back)
        def _():
            for copy in rz(k):
                copy.wait()
            total = Q[here].astype(jnp.float32)
            for i in range(line - 1):
                total = total + RZ[b, i].astype(jnp.float32)
            out[r] = (X[r].astype(jnp.float32) + total).astype(jnp.bfloat16)

            @pl.when(s < sections - 1)
            def _():
                xs(r).start()

        @pl.when(jnp.logical_and(back, s < sections - 1))
        def _():
            xs(r).wait_send()

        return carry

    lax.fori_loop(0, chunks + 2, step, 0)


def per_device(hidden_in, norm_gain, routes, gate_codes, w_gate, w_up, w_down):
    experts = lax.axis_size("expert")
    sections = lax.axis_size("section")
    micro_count, rows, width = hidden_in.shape
    line = experts // 4
    group = ROWS // rows
    chunks = micro_count // group
    hid = w_gate.shape[-1]

    hits = routes[0][..., None] == jnp.arange(LANES, dtype=jnp.int32)
    codes = jnp.sum(jnp.where(hits, gate_codes[0][..., None], 0), axis=2)
    codes = codes.astype(jnp.bfloat16).reshape(chunks, ROWS, LANES)

    bf = jnp.bfloat16
    dma = pltpu.SemaphoreType.DMA
    out = pl.pallas_call(
        functools.partial(moe_kernel, sections, line),
        out_shape=jax.ShapeDtypeStruct((chunks, ROWS, width), bf),
        in_specs=[pl.BlockSpec(memory_space=pltpu.VMEM)] * 3 + [pl.BlockSpec(memory_space=pl.ANY)] * 3,
        out_specs=pl.BlockSpec(memory_space=pltpu.VMEM),
        scratch_shapes=[
            pltpu.VMEM((width, hid), bf), pltpu.VMEM((width, hid), bf), pltpu.VMEM((hid, width), bf),
            dma((3,)),
            pltpu.VMEM((chunks, ROWS, width), bf),
            pltpu.VMEM((3, 2, 2 * line, ROWS, width + LANES), bf),
            pltpu.VMEM((experts * ROWS, hid), bf),
            pltpu.VMEM((2, 2 * line, ROWS, width), bf),
            pltpu.VMEM((2, 2 * line, ROWS, width), bf),
            pltpu.VMEM((2, line, ROWS, width), bf),
            pltpu.VMEM((2, line - 1, ROWS, width), bf),
            pltpu.VMEM((2 * line, ROWS, width), bf),
            dma, dma((chunks,)),
            dma((3, line - 1)), dma((3, line - 1)),
            dma((3,)), dma((3,)), dma((3,)), dma((3,)),
            dma((2,)), dma((2,)), dma((2,)), dma((2,)),
            dma((2, line - 1)), dma((2, line - 1)),
        ],
        compiler_params=pltpu.CompilerParams(
            collective_id=0, has_side_effects=True, vmem_limit_bytes=56 * 2**20
        ),
        cost_estimate=pl.CostEstimate(
            flops=6 * chunks * experts * ROWS * width * hid,
            bytes_accessed=6 * width * hid, transcendentals=0),
    )(hidden_in.reshape(chunks, ROWS, width), norm_gain, codes, w_gate[0, 0], w_up[0, 0], w_down[0, 0])
    return out.reshape(1, micro_count, rows, width)


def solution(mesh):
    return jax.shard_map(
        per_device,
        mesh=mesh,
        in_specs=(
            P(None, "expert", None),
            P("section", None),
            P("section", None, "expert", None),
            P("section", None, "expert", None),
            P("section", "expert", None, None),
            P("section", "expert", None, None),
            P("section", "expert", None, None),
        ),
        out_specs=P("section", None, "expert", None),
        check_vma=False,
    )
```
